32 devices in a mesh: expert: 16 (over z, y, x), tensor: 2 (over core).
Axes of the slice: x: 2, y: 2, z: 4, core: 2. Of those that a mesh axis runs over, the one named last changes fastest.
Arguments:
- tokens: bfloat16 [2048, 7168], P('expert', 'tensor'), may hold values from -6 to 6
- out_grad: bfloat16 [2048, 7168], P('expert', 'tensor'), may hold values from -6 to 6
- gate_weight: bfloat16 [16, 7168, 2048], P('expert', None, 'tensor'), may hold values from -0.0625 to 0.0625
- up_weight: bfloat16 [16, 7168, 2048], P('expert', None, 'tensor'), may hold values from -0.0625 to 0.0625
- proj_hidden: bfloat16 [2048, 64], P('tensor'), may hold values from -0.125 to 0.125
- proj_grad: bfloat16 [7168, 64], P('tensor'), may hold values from -0.0625 to 0.0625
- expert_ids: int32 [2048, 8], P('expert'), may hold values from 0 to 15, all different within a row; in each aligned block of 128 rows (0 to 127, 128 to 255, ...) at most 96 rows name the same one
- weight_index: int32 [2048, 8], P('expert'), may hold values from 0 to 63
- weight_table: float32 [64], replicated, may hold values from 0.02 to 0.4
- sequence_ids: int32 [2048], P('expert'), may hold values from 0 to 3, never falling along the last dimension, each value on 1 to 1024 neighbouring positions
Outputs:
- features: float32 [16, 4, 4096], P('expert', None, 'tensor')
The draws below stay inside these ranges and needn't reach their ends.
Inputs may be any that keep to these rules, and one draw needn't show every extreme that they name: `expert_ids`: within each aligned block of 128 tokens no expert is named by more than 96 tokens, a bound that some block reaches. `sequence_ids`: document ids never fall along the tokens; every document is present.
All inputs are finite; a program needn't handle non-finite values.
Results may differ from the reference program's by a relative error of at most 0.0029.
Values may be sent and summed in bfloat16 or wider, within the bound.
A program may use at most 192 MiB of HBM per device.

```python
import math
import jax
import jax.numpy as jnp
import numpy as np
from jax import lax

D = 7168
FF = 2048
TOPK = 8
R = 64
SEQS = 4
LEVELS = 64
TOK_DEV = 128
EXPERTS = 16
TOKENS = 2048
CAP = 96
N_EXPERT = 16


def place_ends(result, rng, smallest, high):
    index_at = [jax.random.randint(jax.random.fold_in(rng, axis), (), 0, length) for axis, length in enumerate(result.shape)]
    longest = result.shape.index(max(result.shape))
    neighbour = index_at[:longest] + [(index_at[longest] + 1) % result.shape[longest]] + index_at[longest + 1:]
    return result.at[tuple(index_at)].set(smallest).at[tuple(neighbour)].set(high)


def levels(key, dims, shards, low, largest):
    level = 1.0
    for axis_at, blocks in shards:
        heights = jax.random.uniform(jax.random.fold_in(jax.random.fold_in(key, 6), axis_at), (blocks,), jnp.float32, low / len(shards), largest / len(shards))
        level = level * jnp.repeat(jnp.exp(heights), dims[axis_at] // blocks).reshape((-1,) + (1,) * (len(dims) - 1 - axis_at))
    return level


def split_up(number_of, total, bound, skew):
    portions = [(1 << 20) // math.isqrt(rank ** skew) + 1 for rank in range(2, number_of + 1)]
    spare, holding = total - bound - (number_of - 1), [1] * (number_of - 1)
    while spare > 0:
        free = [i for i in range(number_of - 1) if holding[i] < bound]
        mass, budget = sum([portions[i] for i in free]), spare
        for i in free:
            addition = min(bound - holding[i], max(1, budget * portions[i] // mass), spare)
            holding[i] = holding[i] + addition
            spare = spare - addition
    return np.array([bound] + holding)


def uneven_parts(rng, count, total, reach, lean):
    if count == 2:
        one = jax.random.randint(rng, (), max(1, total - reach), min(reach, total - 1) + 1)
        return jnp.stack([one, total - one])
    sizes = jnp.asarray(split_up(count, total, reach, lean), jnp.int32)
    couples = (count - 1) // 2
    giver, receiver = sizes[1:1 + 2 * couples:2], sizes[2:2 + 2 * couples:2]
    room = jnp.minimum(giver - 1, reach - receiver)
    passed = jax.random.randint(jax.random.fold_in(rng, 1), (couples,), 0, 1 << 20) % (room + 1)
    sizes = sizes.at[1:1 + 2 * couples:2].set(giver - passed).at[2:2 + 2 * couples:2].set(receiver + passed)
    return sizes[jax.random.permutation(jax.random.fold_in(rng, 2), count)]


def deal_out(stream_key, own, number, rows, count, top, most, skew):
    sequence = jax.random.permutation(stream_key, count)
    packed, ordinary = load_shares(count, rows * top, most, skew, True), load_shares(count, rows * top, most, skew, False)
    places = jnp.arange(count)

    def named(lengths, offset_by):
        used = int((lengths > 0).sum())
        fixed = max(1, used // 4)
        shifted = fixed + (places - fixed + offset_by * (used - fixed)) % max(1, count - fixed)
        return jnp.zeros((count,), jnp.int32).at[sequence[jnp.where(places < fixed, places, shifted)]].set(jnp.asarray(lengths, jnp.int32))

    lengths = jnp.where(number % 4 == 0, named(packed, number // 4), named(ordinary, number - number // 4 - 1))
    mixed = jax.random.permutation(jax.random.fold_in(own, 3), count)
    giver, taker = mixed[0:count // 2 * 2:2], mixed[1:count // 2 * 2:2]
    margin = jnp.minimum(lengths[giver] - 1, most - lengths[taker]) // 2
    margin = jnp.where((giver == sequence[0]) | (taker == sequence[0]) | (lengths[taker] == 0), 0, jnp.maximum(margin, 0))
    shifted = jax.random.randint(jax.random.fold_in(own, 4), (count // 2,), 0, 1 << 20) % (margin + 1)
    lengths = lengths.at[giver].add(-shifted).at[taker].add(shifted)
    items = jnp.searchsorted(jnp.cumsum(lengths), jnp.arange(rows * top), side="right").astype(jnp.int32)
    listing = items.reshape(top, rows).T
    listing = listing[jax.random.permutation(jax.random.fold_in(own, 1), rows)]
    offset_by = jax.random.randint(jax.random.fold_in(own, 2), (rows, 1), 0, top)
    return jnp.take_along_axis(listing, (jnp.arange(top)[None, :] + offset_by) % top, axis=1)


def load_shares(count, total, reach, lean, full):
    portions = [(1 << 20) // math.isqrt(standing ** lean) + 1 for standing in range(1, count + 1)]
    largest = reach if full else min(reach, max(-(-total // count), total * portions[0] // sum(portions)))
    least = 1 if total - largest >= count - 1 else 0
    counts, rest = [largest] + [least] * (count - 1), total - largest - least * (count - 1)
    while rest > 0:
        candidates = [i for i in range(1, count) if counts[i] < largest] or [i for i in range(1, count) if counts[i] < reach]
        mass, budget = sum([portions[i] for i in candidates]), rest
        for i in candidates:
            addition = min(reach - counts[i], max(1, budget * portions[i] // mass), rest)
            counts[i] = counts[i] + addition
            rest = rest - addition
    return np.array(counts)


def bell_draw(stream_key, extent, deviation, limit, split=(), held_as=jnp.bfloat16):
    array = deviation * jax.random.normal(stream_key, extent, jnp.float32)
    if split:
        array = array * levels(stream_key, extent, split, -0.22, 0.18)
    return jnp.clip(array, -limit, limit).astype(held_as)


def setup_inputs(seed: int = 0) -> dict:
    arg_keys = jax.random.split(jax.random.key(seed), 11)
    tokens = bell_draw(arg_keys[0], (TOKENS, D), 1.0, 6.0, ((0, 16), (1, 2)))
    out_grad = bell_draw(arg_keys[1], (TOKENS, D), 1.0, 6.0, ((0, 16), (1, 2)))
    gate_weight = bell_draw(arg_keys[2], (EXPERTS, D, FF), D ** -0.5, 0.0625, ((0, 16), (2, 2)))
    up_weight = bell_draw(arg_keys[3], (EXPERTS, D, FF), D ** -0.5, 0.0625, ((0, 16), (2, 2)))
    proj_hidden = bell_draw(arg_keys[4], (FF, R), FF ** -0.5, 0.125, ((0, 2),))
    proj_grad = bell_draw(arg_keys[5], (D, R), D ** -0.5, 0.0625, ((0, 2),))
    expert_ids_keys = jax.random.split(jax.random.fold_in(arg_keys[6], 1), TOKENS // TOK_DEV)
    expert_ids_turns = jax.random.permutation(jax.random.fold_in(arg_keys[6], 3), TOKENS // TOK_DEV)
    expert_ids = jax.vmap(lambda own, number: deal_out(jax.random.fold_in(arg_keys[6], 2), own, number, TOK_DEV, EXPERTS, TOPK, CAP, 2))(expert_ids_keys, expert_ids_turns).reshape((TOKENS, TOPK))
    weight_index = place_ends(jax.random.randint(arg_keys[7], (TOKENS, TOPK), 0, LEVELS), jax.random.fold_in(arg_keys[7], 1), 0, LEVELS - 1).astype(jnp.int32)
    weight_table = jnp.clip(jnp.exp(jax.random.uniform(arg_keys[8], (LEVELS,), jnp.float32, math.log(0.02), math.log(0.4))), 0.02, 0.4)
    sequence_ids = jnp.searchsorted(jnp.cumsum(uneven_parts(arg_keys[9], SEQS, TOKENS, 2 * TOKENS // SEQS, 1)), jnp.arange(TOKENS), side="right").astype(jnp.int32)
    return dict(tokens=tokens, out_grad=out_grad, gate_weight=gate_weight, up_weight=up_weight, proj_hidden=proj_hidden, proj_grad=proj_grad, expert_ids=expert_ids, weight_index=weight_index, weight_table=weight_table, sequence_ids=sequence_ids)


def reference(tokens, out_grad, gate_weight, up_weight, proj_hidden, proj_grad, expert_ids, weight_index, weight_table, sequence_ids):
    combine = weight_table[weight_index]
    right_all = jnp.dot(out_grad, proj_grad, preferred_element_type=jnp.float32)
    slots = N_EXPERT * CAP
    pad_tokens = jnp.concatenate([tokens, jnp.zeros((1, D), tokens.dtype)], axis=0)
    pad_right = jnp.concatenate([right_all, jnp.zeros((1, R), right_all.dtype)], axis=0)
    seq_hits = (sequence_ids[:, None] == jnp.arange(SEQS, dtype=jnp.int32)[None, :]).astype(jnp.float32)

    def one_expert(expert):
        hits = expert_ids == expert
        chosen = jnp.any(hits, axis=1)
        weight = jnp.sum(jnp.where(hits, combine, 0.0), axis=1)
        place = jnp.cumsum(chosen.astype(jnp.int32)) - 1
        place = jnp.where(chosen, place, slots).astype(jnp.int32)
        token_list = jnp.full((slots,), TOKENS, jnp.int32).at[place].set(jnp.arange(TOKENS, dtype=jnp.int32), mode="drop")
        rows = pad_tokens[token_list]
        gate_sum = jnp.dot(rows, gate_weight[expert], preferred_element_type=jnp.float32)
        up_sum = jnp.dot(rows, up_weight[expert], preferred_element_type=jnp.float32)
        hidden = (jax.nn.silu(gate_sum) * up_sum).astype(jnp.bfloat16)
        left = jnp.dot(hidden, proj_hidden, preferred_element_type=jnp.float32)
        seq_weight = seq_hits * weight[:, None]
        seq_weight = jnp.concatenate([seq_weight, jnp.zeros((1, SEQS), seq_weight.dtype)], axis=0)[token_list]
        right = pad_right[token_list]
        outer = jnp.einsum("ts,tr,tq->srq", seq_weight, left, right, precision=lax.Precision.HIGHEST)
        return outer.reshape(SEQS, R * R)

    return lax.map(one_expert, jnp.arange(EXPERTS, dtype=jnp.int32))
```

```python
import jax
import jax.numpy as jnp
from jax import lax
from jax.sharding import PartitionSpec as P

SEQS = 4


def small_rows(out_grad, proj_grad, expert_ids, weight_index, weight_table, sequence_ids):
    experts = lax.axis_size("expert")
    right = lax.psum(jnp.dot(out_grad, proj_grad, preferred_element_type=jnp.float32), "tensor")
    levels = jnp.arange(weight_table.shape[0], dtype=jnp.int32)
    combine = jnp.sum(
        jnp.where(weight_index[:, :, None] == levels, weight_table, 0.0), axis=2
    )
    hits = expert_ids[:, :, None] == jnp.arange(experts, dtype=jnp.int32)
    weights = jnp.sum(jnp.where(hits, combine[:, :, None], 0.0), axis=1)
    seq = sequence_ids.astype(jnp.float32)[:, None]
    packed = jnp.concatenate([right, weights, seq], axis=1)
    return lax.all_gather(packed, "expert", axis=0, tiled=True)


def combine_outer(left, packed, experts):
    width = packed.shape[1] - experts - 1
    right = packed[:, :width]
    weight = lax.dynamic_slice_in_dim(packed, width + lax.axis_index("expert"), 1, axis=1)
    seq = packed[:, width + experts :]
    by_seq = jnp.where(seq == jnp.arange(SEQS, dtype=jnp.float32)[None, :], weight, 0.0)
    scaled = (by_seq[:, :, None] * left[:, None, :]).reshape(left.shape[0], -1)
    outer = lax.dot_general(
        scaled, right, (((0,), (0,)), ((), ())), precision=lax.Precision.HIGHEST
    )
    summed = lax.psum_scatter(
        outer.reshape(SEQS, -1), "tensor", scatter_dimension=1, tiled=True
    )
    return summed[None]


def local(
    tokens,
    out_grad,
    gate_weight,
    up_weight,
    proj_hidden,
    proj_grad,
    expert_ids,
    weight_index,
    weight_table,
    sequence_ids,
):
    experts = lax.axis_size("expert")
    packed = small_rows(
        out_grad, proj_grad, expert_ids, weight_index, weight_table, sequence_ids
    )
    rows = lax.all_gather(tokens, "expert", axis=0, tiled=True)
    rows = lax.all_gather(rows, "tensor", axis=1, tiled=True)
    gate_sum = jnp.dot(rows, gate_weight[0], preferred_element_type=jnp.float32)
    up_sum = jnp.dot(rows, up_weight[0], preferred_element_type=jnp.float32)
    hidden = (jax.nn.silu(gate_sum) * up_sum).astype(jnp.bfloat16)
    left = jnp.dot(hidden, proj_hidden, preferred_element_type=jnp.float32)
    return combine_outer(left, packed, experts)


def solution(mesh):
    placed = (
        P("expert", "tensor"),
        P("expert", "tensor"),
        P("expert", None, "tensor"),
        P("expert", None, "tensor"),
        P("tensor", None),
        P("tensor", None),
        P("expert", None),
        P("expert", None),
        P(),
        P("expert"),
    )
    return jax.shard_map(
        local, mesh=mesh, in_specs=placed, out_specs=P("expert", None, "tensor"), check_vma=False
    )
```

```python
import jax
import jax.numpy as jnp
from jax import lax
from jax.experimental import pallas as pl
from jax.experimental.pallas import tpu as pltpu
from jax.sharding import PartitionSpec as P

SEQS = 4


ORDER = (
    "CX0 CY0 CO1 AO1 AX0 AY0 BO1 BY0 BX0 CO2 CD0 CX1 CY1 AX1 AY1 AD0 AO2 BX1 BO2 BD0 AX2 CO3 CD1 "
    "BY1 CX2 CY2 AY2 BX2 AD1 BY2 AO3 AD2 BD1 BD2 BO3 AX3 AY3 CX3 CY3 CD2 BX3 BY3 AD3 BD3 CD3"
).split()
GROUP_ROWS = 256
UNITS = 4
MESH = pl.DeviceIdType.MESH


def part_rows(rows):
    big = rows * 3 // 8 // 16 * 16
    return {"A": (0, big), "B": (big, big), "C": (2 * big, rows - 2 * big)}


def make_groups(spans):
    groups, now, held = [["AO0", "BO0", "CO0"]], [], 0
    for name in ORDER:
        size = spans[name[0]][1]
        if held + size > GROUP_ROWS:
            groups.append(now)
            now, held = [], 0
        now, held = now + [name], held + size
    return groups + [now]


def gather_kernel(
    tok_ref,
    wg_ref,
    wu_ref,
    ph_ref,
    left_ref,
    x,
    wg,
    wu,
    acc,
    recv_sem,
    pair_sem,
    send_sem,
    own_sem,
    weight_sem,
):
    rows, half = tok_ref.shape
    spans = part_rows(rows)
    groups = make_groups(spans)
    cols = wg.shape[1] // UNITS
    me, core = lax.axis_index("expert"), lax.axis_index("tensor")
    mz, my, mx = me // 4, me // 2 % 2, me % 2
    upper = mz // 2
    inner = jnp.where(upper == 1, 3 - mz, mz)

    def reflect(place):
        return jnp.where(upper == 1, 3 - place, place)

    def block_of(name):
        step = int(name[2])
        place = inner if step == 0 else 1 - inner if step == 1 else step
        yy = 1 - my if name[1] in "YD" else my
        xx = 1 - mx if name[1] in "XD" else mx
        return (reflect(place) * 2 + yy) * 2 + xx

    def device(link):
        zz, yy, xx, cc = mz, my, mx, core
        if link == "in":
            zz = reflect(inner + 1)
        elif link == "out":
            zz = reflect(jnp.maximum(inner - 1, 0))
        elif link == "x":
            xx = 1 - mx
        elif link == "y":
            yy = 1 - my
        else:
            cc = 1 - core
        return ((zz * 2 + yy) * 2 + xx, cc)

    def piece(name, which):
        start, size = spans[name[0]]
        return x.at[which, block_of(name), pl.ds(start, size)]

    def sem_index(name):
        return "ABC".index(name[0]) * 16 + block_of(name)

    sent = []

    def send(name, link, when):
        number = len(sent)
        sems = pair_sem if link == "pair" else recv_sem

        def build():
            part = piece(name, core)
            return pltpu.make_async_remote_copy(
                src_ref=part,
                dst_ref=part,
                send_sem=send_sem.at[number],
                recv_sem=sems.at[sem_index(name)],
                device_id=device(link),
                device_id_type=MESH,
            )

        if when is None:
            build().start()
        else:
            pl.when(when)(lambda: build().start())
        sent.append((build, when))

    def sends(name):
        part, column, step = name[0], name[1], int(name[2])
        if column == "O" or part == "C":
            if step == 0:
                send(name, "in", None)
                send(name, "out", inner == 1)
            elif step == 1:
                send(name, "in", inner == 1)
            else:
                send(name, "out", inner == 1)
        if part == "C" and step > 0:
            links = ""
        elif column == "O":
            links = "yx" if part == "B" else "xy"
        elif column == "X":
            links = "" if part == "B" else "y"
        elif column == "Y":
            links = "x" if part == "B" else ""
        else:
            links = ""
        for link in links:
            send(name, link, None)
        send(name, "pair", None)

    def landed(name, which, sems):
        part = piece(name, which)
        pltpu.make_async_remote_copy(
            src_ref=part,
            dst_ref=part,
            send_sem=send_sem.at[0],
            recv_sem=sems.at[sem_index(name)],
            device_id=device("pair"),
            device_id_type=MESH,
        ).wait_recv()

    own = pltpu.make_async_copy(tok_ref, x.at[core, me], own_sem)
    own.start()
    loads = []
    for n in range(UNITS):
        for at, (src, dst) in enumerate(((wg_ref, wg), (wu_ref, wu))):
            load = pltpu.make_async_copy(
                src.at[0, :, pl.ds(n * cols, cols)],
                dst.at[:, pl.ds(n * cols, cols)],
                weight_sem.at[2 * n + at],
            )
            loads.append(load)

    barrier = pltpu.get_barrier_semaphore()
    for link in ("in", "x", "y", "pair"):
        pl.semaphore_signal(barrier, inc=1, device_id=device(link), device_id_type=MESH)

    @pl.when(inner == 1)
    def _():
        pl.semaphore_signal(barrier, inc=1, device_id=device("out"), device_id_type=MESH)

    pl.semaphore_wait(barrier, 4 + inner)
    own.wait()
    for name in ("CO0", "AO0", "BO0"):
        sends(name)
    for load in loads:
        load.start()

    def unit(group, n):
        size = sum(spans[name[0]][1] for name in group)
        if n == 0:
            for name in group:
                landed(name, 1 - core, pair_sem)
        if group[0] == "AO0":
            loads[2 * n].wait()
            loads[2 * n + 1].wait()
        blocks = [(block_of(name),) + spans[name[0]] for name in group]
        wide = pl.ds(n * cols, cols)

        def step(i, carry):
            lanes = pl.ds(pl.multiple_of(i % 2 * (half // 2), 128), half // 2)
            deep = pl.ds(pl.multiple_of(i * (half // 2), 128), half // 2)
            lhs = jnp.concatenate(
                [x[i // 2, at, pl.ds(start, count), lanes] for at, start, count in blocks], axis=0
            )
            gate = jnp.dot(lhs, wg[deep, wide], preferred_element_type=jnp.float32)
            up = jnp.dot(lhs, wu[deep, wide], preferred_element_type=jnp.float32)
            acc[0, pl.ds(0, size)] = jnp.where(i > 0, acc[0, pl.ds(0, size)], 0.0) + gate
            acc[1, pl.ds(0, size)] = jnp.where(i > 0, acc[1, pl.ds(0, size)], 0.0) + up
            return carry

        lax.fori_loop(0, 4, step, 0)
        gate, up = acc[0, pl.ds(0, size)], acc[1, pl.ds(0, size)]
        hidden = (gate / (1.0 + jnp.exp(-gate)) * up).astype(jnp.bfloat16)
        part = jnp.dot(hidden, ph_ref[wide], preferred_element_type=jnp.float32)
        done = 0
        for at, start, count in blocks:
            piece_rows = part[done : done + count]
            if n > 0:
                piece_rows = piece_rows + left_ref[at, pl.ds(start, count)]
            left_ref[at, pl.ds(start, count)] = piece_rows
            done += count

    for g in range(1, len(groups) + 1):
        waiting = list(groups[g]) if g < len(groups) else []
        per = -(-len(waiting) // UNITS)
        for n in range(UNITS):
            unit(groups[g - 1], n)
            for name in waiting[n * per : (n + 1) * per]:
                landed(name, core, recv_sem)
                sends(name)

    for build, when in sent:
        if when is None:
            build().wait_send()
        else:
            pl.when(when)(lambda build=build: build().wait_send())


def count_sends():
    total = 0
    for name in ["AO0", "BO0", "CO0"] + ORDER:
        part, column, step = name[0], name[1], int(name[2])
        if column == "O" or part == "C":
            total += 2 if step == 0 else 1
        if not (part == "C" and step > 0):
            total += {"O": 2, "X": int(part != "B"), "Y": int(part == "B"), "D": 0}[column]
        total += 1
    return total


def gathered_left(tokens, gate_weight, up_weight, proj_hidden):
    experts = lax.axis_size("expert")
    rows, half = tokens.shape
    _, deep, wide = gate_weight.shape
    width = proj_hidden.shape[1]
    left = pl.pallas_call(
        gather_kernel,
        out_shape=jax.ShapeDtypeStruct((experts, rows, width), jnp.float32),
        in_specs=[pl.BlockSpec(memory_space=pl.ANY)] * 3
        + [pl.BlockSpec(memory_space=pltpu.VMEM)],
        out_specs=pl.BlockSpec(memory_space=pltpu.VMEM),
        scratch_shapes=[
            pltpu.VMEM((2, experts, rows, half), jnp.bfloat16),
            pltpu.VMEM((deep, wide), jnp.bfloat16),
            pltpu.VMEM((deep, wide), jnp.bfloat16),
            pltpu.VMEM((2, GROUP_ROWS, wide // UNITS), jnp.float32),
            pltpu.SemaphoreType.DMA((3 * experts,)),
            pltpu.SemaphoreType.DMA((3 * experts,)),
            pltpu.SemaphoreType.DMA((count_sends(),)),
            pltpu.SemaphoreType.DMA,
            pltpu.SemaphoreType.DMA((2 * UNITS,)),
        ],
        compiler_params=pltpu.CompilerParams(
            collective_id=0, has_side_effects=True, vmem_limit_bytes=62 * 2**20
        ),
        cost_estimate=pl.CostEstimate(
            flops=4 * experts * rows * deep * wide,
            bytes_accessed=4 * deep * wide + 2 * rows * half,
            transcendentals=experts * rows * wide,
        ),
    )(tokens, gate_weight, up_weight, proj_hidden)
    return left.reshape(experts * rows, width)


def small_rows(out_grad, proj_grad, expert_ids, weight_index, weight_table, sequence_ids):
    experts = lax.axis_size("expert")
    right = lax.psum(jnp.dot(out_grad, proj_grad, preferred_element_type=jnp.float32), "tensor")
    levels = jnp.arange(weight_table.shape[0], dtype=jnp.int32)
    combine = jnp.sum(
        jnp.where(weight_index[:, :, None] == levels, weight_table, 0.0), axis=2
    )
    hits = expert_ids[:, :, None] == jnp.arange(experts, dtype=jnp.int32)
    weights = jnp.sum(jnp.where(hits, combine[:, :, None], 0.0), axis=1)
    seq = sequence_ids.astype(jnp.float32)[:, None]
    packed = jnp.concatenate([right, weights, seq], axis=1)
    return lax.all_gather(packed, "expert", axis=0, tiled=True)


def combine_outer(left, packed, experts):
    width = packed.shape[1] - experts - 1
    right = packed[:, :width]
    weight = lax.dynamic_slice_in_dim(packed, width + lax.axis_index("expert"), 1, axis=1)
    seq = packed[:, width + experts :]
    by_seq = jnp.where(seq == jnp.arange(SEQS, dtype=jnp.float32)[None, :], weight, 0.0)
    scaled = (by_seq[:, :, None] * left[:, None, :]).reshape(left.shape[0], -1)
    outer = lax.dot_general(
        scaled, right, (((0,), (0,)), ((), ())), precision=lax.Precision.HIGHEST
    )
    summed = lax.psum_scatter(
        outer.reshape(SEQS, -1), "tensor", scatter_dimension=1, tiled=True
    )
    return summed[None]


def local(
    tokens,
    out_grad,
    gate_weight,
    up_weight,
    proj_hidden,
    proj_grad,
    expert_ids,
    weight_index,
    weight_table,
    sequence_ids,
):
    experts = lax.axis_size("expert")
    packed = small_rows(
        out_grad, proj_grad, expert_ids, weight_index, weight_table, sequence_ids
    )
    if experts == 16 and lax.axis_size("tensor") == 2:
        left = gathered_left(tokens, gate_weight, up_weight, proj_hidden)
        return combine_outer(left, packed, experts)
    rows = lax.all_gather(tokens, "expert", axis=0, tiled=True)
    rows = lax.all_gather(rows, "tensor", axis=1, tiled=True)
    gate_sum = jnp.dot(rows, gate_weight[0], preferred_element_type=jnp.float32)
    up_sum = jnp.dot(rows, up_weight[0], preferred_element_type=jnp.float32)
    hidden = (jax.nn.silu(gate_sum) * up_sum).astype(jnp.bfloat16)
    left = jnp.dot(hidden, proj_hidden, preferred_element_type=jnp.float32)
    return combine_outer(left, packed, experts)


def solution(mesh):
    placed = (
        P("expert", "tensor"),
        P("expert", "tensor"),
        P("expert", None, "tensor"),
        P("expert", None, "tensor"),
        P("tensor", None),
        P("tensor", None),
        P("expert", None),
        P("expert", None),
        P(),
        P("expert"),
    )
    return jax.shard_map(
        local, mesh=mesh, in_specs=placed, out_specs=P("expert", None, "tensor"), check_vma=False
    )
```

```python
import jax
import jax.numpy as jnp
from jax import lax
from jax.experimental import pallas as pl
from jax.experimental.pallas import tpu as pltpu
from jax.sharding import PartitionSpec as P

SEQS = 4


ORDER = (
    "CX0", "CY0", "CO1", "AO1", "AX0", "AY0", "BO1", "SO1", "BY0", "SY0", "BX0", "SX0", "CO2",
    "CD0", "CX1", "CY1", "AX1", "AY1", "AD0", "AO2", "BX1", "SX1", "BO2", "SO2", "BD0", "SD0",
    "AX2", "CO3", "CD1", "BY1", "SY1", "CX2", "CY2", "AY2", "BX2", "SX2", "AD1", "BY2", "SY2",
    "AO3", "AD2", "BD1", "SD1", "BD2", "SD2", "BO3", "SO3", "AX3", "AY3", "CX3", "CY3", "CD2",
    "BX3", "SX3", "BY3", "SY3", "AD3", "BD3", "SD3", "CD3",
)
GROUP_ROWS = (256, 512, 512, 384, 256)
UNITS = 4
MESH = pl.DeviceIdType.MESH


def part_rows(rows):
    big = rows * 3 // 8 // 16 * 16
    return {"A": (0, big), "B": (big, big), "C": (2 * big, rows - 2 * big)}


def make_groups(spans):
    groups, sizes, now, held = [["AO0", "BO0", "CO0"]], list(GROUP_ROWS), [], 0
    for name in ORDER:
        size = spans[name[0]][1] if name[0] != "S" else 0
        if held + size > sizes[0] and len(sizes) > 1:
            groups.append(now)
            now, held = [], 0
            sizes.pop(0)
        now, held = now + [name], held + size
    return groups + [now]


def most_rows(spans):
    return max(
        sum(spans[name[0]][1] for name in group if name[0] != "S") for group in make_groups(spans)
    )


def gather_kernel(
    tok_ref,
    wg_ref,
    wu_ref,
    ph_ref,
    small_ref,
    out_ref,
    left_ref,
    x,
    wg,
    wu,
    acc,
    small,
    partner,
    full,
    other,
    recv_sem,
    pair_sem,
    send_sem,
    own_sem,
    weight_sem,
    swap_sem,
):
    rows, half = tok_ref.shape
    spans = part_rows(rows)
    groups = make_groups(spans)
    cols = wg.shape[1] // UNITS
    me, core = lax.axis_index("expert"), lax.axis_index("tensor")
    mz, my, mx = me // 4, me // 2 % 2, me % 2
    upper = mz // 2
    inner = jnp.where(upper == 1, 3 - mz, mz)

    def reflect(place):
        return jnp.where(upper == 1, 3 - place, place)

    def block_of(name):
        step = int(name[2])
        place = inner if step == 0 else 1 - inner if step == 1 else step
        yy = 1 - my if name[1] in "YD" else my
        xx = 1 - mx if name[1] in "XD" else mx
        return (reflect(place) * 2 + yy) * 2 + xx

    def device(link):
        zz, yy, xx, cc = mz, my, mx, core
        if link == "in":
            zz = reflect(inner + 1)
        elif link == "out":
            zz = reflect(jnp.maximum(inner - 1, 0))
        elif link == "x":
            xx = 1 - mx
        elif link == "y":
            yy = 1 - my
        else:
            cc = 1 - core
        return ((zz * 2 + yy) * 2 + xx, cc)

    def piece(name, which):
        if name[0] == "S":
            return small.at[block_of(name), pl.ds(which * (rows // 2), rows // 2)]
        start, size = spans[name[0]]
        return x.at[which, block_of(name), pl.ds(start, size)]

    def sem_index(name):
        return "ABCS".index(name[0]) * 16 + block_of(name)

    sent = []

    def send(name, link, when):
        number = len(sent)
        sems = pair_sem if link == "pair" else recv_sem

        def build():
            part = piece(name, core)
            return pltpu.make_async_remote_copy(
                src_ref=part,
                dst_ref=part,
                send_sem=send_sem.at[number],
                recv_sem=sems.at[sem_index(name)],
                device_id=device(link),
                device_id_type=MESH,
            )

        if when is None:
            build().start()
        else:
            pl.when(when)(lambda: build().start())
        sent.append((build, when))

    def sends(name):
        part, column, step = name[0], name[1], int(name[2])
        if column == "O" or part == "C":
            if step == 0:
                send(name, "in", None)
                send(name, "out", inner == 1)
            elif step == 1:
                send(name, "in", inner == 1)
            else:
                send(name, "out", inner == 1)
        if part == "C" and step > 0:
            links = ""
        elif column == "O":
            links = "yx" if part in "BS" else "xy"
        elif column == "X":
            links = "" if part in "BS" else "y"
        elif column == "Y":
            links = "x" if part in "BS" else ""
        else:
            links = ""
        for link in links:
            send(name, link, None)
        send(name, "pair", None)

    def landed(name, which, sems):
        part = piece(name, which)
        pltpu.make_async_remote_copy(
            src_ref=part,
            dst_ref=part,
            send_sem=send_sem.at[0],
            recv_sem=sems.at[sem_index(name)],
            device_id=device("pair"),
            device_id_type=MESH,
        ).wait_recv()

    own = pltpu.make_async_copy(tok_ref, x.at[core, me], own_sem)
    own.start()
    loads = []
    for n in range(UNITS):
        for at, (src, dst) in enumerate(((wg_ref, wg), (wu_ref, wu))):
            load = pltpu.make_async_copy(
                src.at[0, :, pl.ds(n * cols, cols)],
                dst.at[:, pl.ds(n * cols, cols)],
                weight_sem.at[2 * n + at],
            )
            loads.append(load)

    barrier = pltpu.get_barrier_semaphore()
    for link in ("in", "x", "y", "pair"):
        pl.semaphore_signal(barrier, inc=1, device_id=device(link), device_id_type=MESH)

    @pl.when(inner == 1)
    def _():
        pl.semaphore_signal(barrier, inc=1, device_id=device("out"), device_id_type=MESH)

    pl.semaphore_wait(barrier, 4 + inner)

    def swap(src, dst, number):
        return pltpu.make_async_remote_copy(
            src_ref=src,
            dst_ref=dst,
            send_sem=swap_sem.at[2 * number],
            recv_sem=swap_sem.at[2 * number + 1],
            device_id=device("pair"),
            device_id_type=MESH,
        )

    share = rows // 2
    mine = pl.ds(pl.multiple_of(core * share, share), share)
    theirs = pl.ds(pl.multiple_of((1 - core) * share, share), share)
    partial = swap(small_ref.at[theirs], partner, 0)
    partial.start()
    own.wait()
    for name in ("CO0", "AO0", "BO0"):
        sends(name)
    partial.wait()
    small[me, mine] = small_ref[mine] + partner[...]
    sends("SO0")
    for load in loads:
        load.start()

    def unit(group, n, handle):
        group = [name for name in group if name[0] != "S"]
        size = sum(spans[name[0]][1] for name in group)
        if n == 0:
            for name in group:
                landed(name, 1 - core, pair_sem)
        if group[0] == "AO0":
            loads[2 * n].wait()
            loads[2 * n + 1].wait()
        blocks = [(block_of(name),) + spans[name[0]] for name in group]
        wide = pl.ds(n * cols, cols)

        def step(i, carry):
            lanes = pl.ds(pl.multiple_of(i % 2 * (half // 2), 128), half // 2)
            deep = pl.ds(pl.multiple_of(i * (half // 2), 128), half // 2)
            lhs = jnp.concatenate(
                [x[i // 2, at, pl.ds(start, count), lanes] for at, start, count in blocks], axis=0
            )
            gate = jnp.dot(lhs, wg[deep, wide], preferred_element_type=jnp.float32)
            up = jnp.dot(lhs, wu[deep, wide], preferred_element_type=jnp.float32)
            acc[0, pl.ds(0, size)] = jnp.where(i > 0, acc[0, pl.ds(0, size)], 0.0) + gate
            acc[1, pl.ds(0, size)] = jnp.where(i > 0, acc[1, pl.ds(0, size)], 0.0) + up
            return carry

        lax.fori_loop(0, 2, step, 0)
        handle()
        lax.fori_loop(2, 4, step, 0)
        gate, up = acc[0, pl.ds(0, size)], acc[1, pl.ds(0, size)]
        hidden = (gate / (1.0 + jnp.exp(-gate)) * up).astype(jnp.bfloat16)
        part = jnp.dot(hidden, ph_ref[wide], preferred_element_type=jnp.float32)
        done = 0
        for at, start, count in blocks:
            piece_rows = part[done : done + count]
            if n > 0:
                piece_rows = piece_rows + left_ref[at, pl.ds(start, count)]
            left_ref[at, pl.ds(start, count)] = piece_rows
            done += count
        handle()

    for g in range(1, len(groups) + 1):
        waiting = list(groups[g]) if g < len(groups) else []
        per = -(-len(waiting) // (2 * UNITS))

        def handle():
            for name in waiting[:per]:
                landed(name, core, recv_sem)
                sends(name)
            del waiting[:per]

        for n in range(UNITS):
            unit(groups[g - 1], n, handle)

    for name in ("SO0",) + ORDER:
        if name[0] == "S":
            landed(name, 1 - core, pair_sem)
    width = left_ref.shape[2]
    experts = x.shape[1]
    together = 4

    def outer(i, carry):
        held = pl.ds(i * together, together)
        packed = small[held].reshape(together * rows, small.shape[2])
        left = left_ref[held].reshape(together * rows, width)
        lane = lax.broadcasted_iota(jnp.int32, packed.shape, 1)
        weight = jnp.sum(jnp.where(lane == width + me, packed, 0.0), axis=1, keepdims=True)
        seq = packed[:, width + experts : width + experts + 1]
        for s in range(SEQS):
            scaled = left * jnp.where(seq == float(s), weight, 0.0)
            term = lax.dot_general(
                scaled,
                packed,
                (((0,), (0,)), ((), ())),
                precision=lax.Precision.HIGHEST,
                preferred_element_type=jnp.float32,
            )
            full[s] = jnp.where(i > 0, full[s], 0.0) + term
        return carry

    lax.fori_loop(0, experts // together, outer, 0)
    share = width // 2
    mine = pl.ds(pl.multiple_of(core * share, share), share)
    theirs = pl.ds(pl.multiple_of((1 - core) * share, share), share)
    last = swap(full.at[:, theirs], other, 1)
    last.start()
    last.wait()
    out_ref[...] = (full[:, mine] + other[...])[:, :, :width]

    for build, when in sent:
        if when is None:
            build().wait_send()
        else:
            pl.when(when)(lambda build=build: build().wait_send())


def count_sends():
    total = 0
    for name in ("AO0", "BO0", "CO0", "SO0") + ORDER:
        part, column, step = name[0], name[1], int(name[2])
        if column == "O" or part == "C":
            total += 2 if step == 0 else 1
        if not (part == "C" and step > 0):
            total += {"O": 2, "X": int(part not in "BS"), "Y": int(part in "BS"), "D": 0}[column]
        total += 1
    return total


def gathered_features(tokens, gate_weight, up_weight, proj_hidden, small):
    experts = lax.axis_size("expert")
    rows, half = tokens.shape
    _, deep, wide = gate_weight.shape
    width = proj_hidden.shape[1]
    lanes = small.shape[1]
    f32, bf16 = jnp.float32, jnp.bfloat16
    return pl.pallas_call(
        gather_kernel,
        out_shape=jax.ShapeDtypeStruct((SEQS, width // 2, width), f32),
        in_specs=[pl.BlockSpec(memory_space=pl.ANY)] * 3
        + [pl.BlockSpec(memory_space=pltpu.VMEM)] * 2,
        out_specs=pl.BlockSpec(memory_space=pltpu.VMEM),
        scratch_shapes=[
            pltpu.VMEM((experts, rows, width), f32),
            pltpu.VMEM((2, experts, rows, half), bf16),
            pltpu.VMEM((deep, wide), bf16),
            pltpu.VMEM((deep, wide), bf16),
            pltpu.VMEM((2, most_rows(part_rows(rows)), wide // UNITS), f32),
            pltpu.VMEM((experts, rows, lanes), f32),
            pltpu.VMEM((rows // 2, lanes), f32),
            pltpu.VMEM((SEQS, width, lanes), f32),
            pltpu.VMEM((SEQS, width // 2, lanes), f32),
            pltpu.SemaphoreType.DMA((4 * experts,)),
            pltpu.SemaphoreType.DMA((4 * experts,)),
            pltpu.SemaphoreType.DMA((count_sends(),)),
            pltpu.SemaphoreType.DMA,
            pltpu.SemaphoreType.DMA((2 * UNITS,)),
            pltpu.SemaphoreType.DMA((4,)),
        ],
        compiler_params=pltpu.CompilerParams(
            collective_id=0, has_side_effects=True, vmem_limit_bytes=62 * 2**20
        ),
        cost_estimate=pl.CostEstimate(
            flops=4 * experts * rows * deep * wide,
            bytes_accessed=4 * deep * wide + 2 * rows * half,
            transcendentals=experts * rows * wide,
        ),
    )(tokens, gate_weight, up_weight, proj_hidden, small)


def small_rows(expert_ids, weight_index, weight_table, sequence_ids):
    experts = lax.axis_size("expert")
    levels = jnp.arange(weight_table.shape[0], dtype=jnp.int32)
    combine = jnp.sum(
        jnp.where(weight_index[:, :, None] == levels, weight_table, 0.0), axis=2
    )
    hits = expert_ids[:, :, None] == jnp.arange(experts, dtype=jnp.int32)
    weights = jnp.sum(jnp.where(hits, combine[:, :, None], 0.0), axis=1)
    return jnp.concatenate([weights, sequence_ids.astype(jnp.float32)[:, None]], axis=1)


def combine_outer(left, packed, experts):
    width = packed.shape[1] - experts - 1
    right = packed[:, :width]
    weight = lax.dynamic_slice_in_dim(packed, width + lax.axis_index("expert"), 1, axis=1)
    seq = packed[:, width + experts :]
    by_seq = jnp.where(seq == jnp.arange(SEQS, dtype=jnp.float32)[None, :], weight, 0.0)
    scaled = (by_seq[:, :, None] * left[:, None, :]).reshape(left.shape[0], -1)
    outer = lax.dot_general(
        scaled, right, (((0,), (0,)), ((), ())), precision=lax.Precision.HIGHEST
    )
    summed = lax.psum_scatter(
        outer.reshape(SEQS, -1), "tensor", scatter_dimension=1, tiled=True
    )
    return summed[None]


def local(
    tokens,
    out_grad,
    gate_weight,
    up_weight,
    proj_hidden,
    proj_grad,
    expert_ids,
    weight_index,
    weight_table,
    sequence_ids,
):
    experts = lax.axis_size("expert")
    small = small_rows(expert_ids, weight_index, weight_table, sequence_ids)
    right = jnp.dot(out_grad, proj_grad, preferred_element_type=jnp.float32)
    if experts == 16 and lax.axis_size("tensor") == 2:
        small = jnp.where(lax.axis_index("tensor") == 0, small, 0.0)
        packed = jnp.concatenate([right, small], axis=1)
        packed = jnp.pad(packed, ((0, 0), (0, -packed.shape[1] % 128)))
        features = gathered_features(tokens, gate_weight, up_weight, proj_hidden, packed)
        return features.reshape(1, SEQS, -1)
    packed = jnp.concatenate([lax.psum(right, "tensor"), small], axis=1)
    packed = lax.all_gather(packed, "expert", axis=0, tiled=True)
    rows = lax.all_gather(tokens, "expert", axis=0, tiled=True)
    rows = lax.all_gather(rows, "tensor", axis=1, tiled=True)
    gate_sum = jnp.dot(rows, gate_weight[0], preferred_element_type=jnp.float32)
    up_sum = jnp.dot(rows, up_weight[0], preferred_element_type=jnp.float32)
    hidden = (jax.nn.silu(gate_sum) * up_sum).astype(jnp.bfloat16)
    left = jnp.dot(hidden, proj_hidden, preferred_element_type=jnp.float32)
    return combine_outer(left, packed, experts)


def solution(mesh):
    placed = (
        P("expert", "tensor"),
        P("expert", "tensor"),
        P("expert", None, "tensor"),
        P("expert", None, "tensor"),
        P("tensor", None),
        P("tensor", None),
        P("expert", None),
        P("expert", None),
        P(),
        P("expert"),
    )
    return jax.shard_map(
        local, mesh=mesh, in_specs=placed, out_specs=P("expert", None, "tensor"), check_vma=False
    )
```
